32 devices in a mesh: ctx: 8 (over y, x, core), head: 4 (over z).
Axes of the slice: x: 2, y: 2, z: 4, core: 2. Of those that a mesh axis runs over, the one named last changes fastest.
Arguments:
- queries: bfloat16 [2048, 4096], P('ctx', 'head'), may hold values from -6 to 6
- keys_values: bfloat16 [2048, 1024], P('ctx'), may hold values from -6 to 6
- grad_rows: bfloat16 [2048, 2880], P('ctx', 'head'), may hold values from -6 to 6
- doc_ids: int32 [2048], replicated, may hold values from 0 to 7, never falling along the last dimension, each value on 1 to 512 neighbouring positions
- tile_list: int32 [16], replicated, may hold values from 0 to 15, each once
Outputs:
- attended: float32 [2048, 4096], P('ctx', 'head')
- weight_grad: float32 [2880, 4096], P('ctx', 'head')
The draws below stay inside these ranges and needn't reach their ends.
Inputs may be any that keep to these rules, and one draw needn't show every extreme that they name: `tile_list`: every slot index names a different tile. `doc_ids`: never falling along the window; each document holds 1 to 512 positions.
All inputs are finite; a program needn't handle non-finite values.
Results may differ from the reference program's by a relative error of at most 0.0018.
Values may be sent and summed in bfloat16 or wider, within the bound.
A program may use at most 128 MiB of HBM per device.

```python
import math
import jax
import jax.numpy as jnp
import numpy as np
from jax import lax

D = 2880
H = 64
KVH = 8
DH = 64
TILE = 128
TOKENS = 2048


def draw_queries(key, part):
    base = jnp.clip(1.5 * jax.random.normal(jax.random.fold_in(key, 1), (TOKENS, H * DH), jnp.float32), -6.0, 6.0)
    return base.astype(jnp.bfloat16)


def draw_keys_values(key, part):
    base = jnp.clip(jax.random.normal(jax.random.fold_in(key, 4), (TOKENS, KVH, 2, DH), jnp.float32), -6.0, 6.0)
    return base.reshape(TOKENS, KVH * 2 * DH).astype(jnp.bfloat16)


def strengthened(values, key, source, target, shards_of, factor):
    def block_of(position):
        return (jnp.arange(values.shape[position]) // (values.shape[position] // shards_of)).reshape((-1,) + (1,) * (values.ndim - 1 - position))

    one_side = jax.random.permutation(key, shards_of)[block_of(target)]
    far = (block_of(target) + shards_of // 2) % shards_of
    return jnp.where((block_of(source) == one_side) | (block_of(source) == far), factor * values, values)


def shard_levels(key, extent, pieces, least, high):
    def one(dim, blocks):
        steps = jax.random.uniform(jax.random.fold_in(jax.random.fold_in(key, 6), dim), (blocks,), jnp.float32, least / len(pieces), high / len(pieces))
        return jnp.repeat(jnp.exp(steps), extent[dim] // blocks).reshape((-1,) + (1,) * (len(extent) - dim - 1))

    gain = one(*pieces[0])
    for cut in pieces[1:]:
        gain = gain * one(*cut)
    return gain


def split_up(number_of, total, bound, slope):
    portions = [(1 << 20) // math.isqrt(standing ** slope) + 1 for standing in range(2, number_of + 1)]
    rest, counts = total - bound - (number_of - 1), [1] * (number_of - 1)
    while rest > 0:
        free = [i for i in range(number_of - 1) if counts[i] < bound]
        whole, remaining = sum([portions[i] for i in free]), rest
        for i in free:
            more = min(bound - counts[i], max(1, remaining * portions[i] // whole), rest)
            counts[i] = counts[i] + more
            rest = rest - more
    return np.array([bound] + counts)


def ragged(own_key, amount, total, bound, lean):
    if amount == 2:
        one = jax.random.randint(own_key, (), max(1, total - bound), min(bound, total - 1) + 1)
        return jnp.stack([one, total - one])
    tallies = jnp.asarray(split_up(amount, total, bound, lean), jnp.int32)
    couples = (amount - 1) // 2
    donor, receiver = tallies[1:1 + 2 * couples:2], tallies[2:2 + 2 * couples:2]
    margin = jnp.minimum(donor - 1, bound - receiver)
    moved = jax.random.randint(jax.random.fold_in(own_key, 1), (couples,), 0, 1 << 20) % (margin + 1)
    tallies = tallies.at[1:1 + 2 * couples:2].set(donor - moved).at[2:2 + 2 * couples:2].set(receiver + moved)
    return tallies[jax.random.permutation(jax.random.fold_in(own_key, 2), amount)]


def noise_with(own_key, dims, deviation, bound, pieces, heavy, kind=jnp.bfloat16):
    drawn = deviation * jax.random.normal(own_key, dims, jnp.float32)
    if pieces:
        drawn = drawn * shard_levels(own_key, dims, pieces, -0.22, 0.18)
    return jnp.clip(strengthened(drawn, jax.random.fold_in(own_key, 3), *heavy), -bound, bound).astype(kind)


def setup_inputs(seed: int = 0) -> dict:
    key_of = jax.random.split(jax.random.key(seed), 6)
    queries = draw_queries(jax.random.fold_in(key_of[5], 71), 0)
    keys_values = draw_keys_values(jax.random.fold_in(key_of[5], 71), 0)
    grad_rows = noise_with(key_of[2], (TOKENS, D), 1.0, 6.0, ((0, 8), (1, 4)), (0, 1, 8, 2.0))
    doc_ids = jnp.searchsorted(jnp.cumsum(ragged(key_of[3], 8, TOKENS, TOKENS // 4, 1)), jnp.arange(TOKENS), side="right").astype(jnp.int32)
    tile_list = jax.random.permutation(key_of[4], TOKENS // TILE).astype(jnp.int32)
    return dict(queries=queries, keys_values=keys_values, grad_rows=grad_rows, doc_ids=doc_ids, tile_list=tile_list)


NEG_FILL = -1e30


def reference(queries, keys_values, grad_rows, doc_ids, tile_list):
    total = queries.shape[0]
    group = H // KVH
    scale = DH ** -0.5
    offsets = jnp.arange(TILE, dtype=jnp.int32)
    slot_pos = (tile_list[:, None] * TILE + offsets[None, :]).reshape(-1).astype(jnp.int32)
    slot_doc = doc_ids.reshape(-1, TILE)[tile_list].reshape(-1)
    blocks = keys_values.reshape(total, KVH, 2, DH).astype(jnp.float32)
    keys = blocks[:, :, 0]
    values = blocks[:, :, 1]
    grouped = queries.reshape(total, KVH, group, DH)
    rows = math.gcd(512, total)
    count = total // rows

    def one_block(index):
        start = (index * rows).astype(jnp.int32)
        query_pos = lax.dynamic_slice_in_dim(slot_pos, start, rows)
        query_doc = lax.dynamic_slice_in_dim(slot_doc, start, rows)
        allowed = (query_doc[:, None] == slot_doc[None, :]) & (slot_pos[None, :] <= query_pos[:, None])
        query_block = lax.dynamic_slice_in_dim(grouped, start, rows).astype(jnp.float32)

        def one_head(kv_head):
            query_head = query_block[:, kv_head]
            scores = jnp.einsum("tqd,nd->qtn", query_head, keys[:, kv_head]) * scale
            masked = jnp.where(allowed[None], scores, NEG_FILL)
            top = jnp.max(masked, axis=-1, keepdims=True)
            weights = jnp.where(allowed[None], jnp.exp(masked - top), 0.0)
            denom = jnp.sum(weights, axis=-1)
            rounded = lax.optimization_barrier(weights.astype(jnp.bfloat16)).astype(jnp.float32)
            summed = jnp.einsum("qtn,nd->tqd", rounded, values[:, kv_head])
            return summed / jnp.transpose(denom)[..., None]

        heads_out = lax.map(one_head, jnp.arange(KVH, dtype=jnp.int32))
        return jnp.transpose(heads_out, (1, 0, 2, 3)).reshape(rows, H * DH)

    attended = lax.map(one_block, jnp.arange(count, dtype=jnp.int32)).reshape(total, H * DH)
    weight_grad = jnp.dot(grad_rows.astype(jnp.float32).T, attended,
                          precision=lax.Precision.HIGHEST, preferred_element_type=jnp.float32)
    return attended, weight_grad
```

```python
import functools
import jax
import jax.numpy as jnp
from jax import lax
from jax.experimental import pallas as pl
from jax.experimental.pallas import tpu as pltpu
from jax.sharding import PartitionSpec as P

H = 64
KVH = 8
DH = 64
TILE = 128

NEG_FILL = -1e30


def attend_kernel(pairs, lo_ref, hi_ref, slot_ref, q_ref, kv_ref, start_ref, pos_ref,
                  out_ref, low_ref, s_ref, m_ref, l_ref, o_ref):
    t = pl.program_id(0)
    lo = lo_ref[t]
    hi = hi_ref[t]
    lane = lax.broadcasted_iota(jnp.int32, (TILE, TILE), 1)
    first = lane < DH
    q = jnp.concatenate(
        [q_ref[:, 2 * DH * i:2 * DH * (i + 1)] for i in range(pairs)], axis=0
    ) * jnp.bfloat16(DH ** -0.5)
    start = start_ref[...]
    pos = pos_ref[...]

    def tile_of(p):
        kv = kv_ref[pl.ds(pl.multiple_of(slot_ref[p] * TILE, TILE), TILE), :].astype(jnp.float32)
        return kv, pltpu.roll(kv, DH, 1)

    m_ref[...] = jnp.full_like(m_ref, NEG_FILL)

    @pl.loop(lo, hi + 1)
    def _(p):
        kv, swapped = tile_of(p)
        keys = jnp.concatenate(
            [jnp.where(first, kv, 0.0), jnp.where(first, 0.0, swapped)], axis=0
        ).astype(jnp.bfloat16)
        s = lax.dot_general(q, keys, (((1,), (1,)), ((), ())), preferred_element_type=jnp.float32)
        at = p * TILE + lane
        bias = jnp.where((at >= start) & (at <= pos), 0.0, NEG_FILL)
        bias = jnp.concatenate([bias, bias], axis=1)
        s = s + jnp.concatenate([bias] * pairs, axis=0)
        s_ref[p - lo] = s
        m_ref[...] = jnp.maximum(m_ref[...], s)

    m_even = jnp.max(m_ref[:, :TILE], axis=1, keepdims=True)
    m_odd = jnp.max(m_ref[:, TILE:], axis=1, keepdims=True)
    m_ref[:, :TILE] = jnp.broadcast_to(m_even, (pairs * TILE, TILE))
    m_ref[:, TILE:] = jnp.broadcast_to(m_odd, (pairs * TILE, TILE))
    l_ref[...] = jnp.zeros_like(l_ref)
    o_ref[...] = jnp.zeros_like(o_ref)

    @pl.loop(lo, hi + 1)
    def _(p):
        kv, swapped = tile_of(p)
        values = jnp.concatenate(
            [jnp.where(first, swapped, 0.0), jnp.where(first, 0.0, kv)], axis=0
        ).astype(jnp.bfloat16)
        w = jnp.exp(s_ref[p - lo] - m_ref[...])
        l_ref[...] += w
        o_ref[...] += jnp.dot(w.astype(jnp.bfloat16), values, preferred_element_type=jnp.float32)

    l_even = jnp.sum(l_ref[:, :TILE], axis=1, keepdims=True)
    l_odd = jnp.sum(l_ref[:, TILE:], axis=1, keepdims=True)
    wide = lax.broadcasted_iota(jnp.int32, (pairs * TILE, TILE), 1)
    o = o_ref[...] / jnp.where(wide < DH, l_even, l_odd)
    for i in range(pairs):
        part = o[i * TILE:(i + 1) * TILE]
        out_ref[:, 2 * DH * i:2 * DH * (i + 1)] = part
        low_ref[:, 2 * DH * i:2 * DH * (i + 1)] = part.astype(jnp.bfloat16)


def attend(queries, kv, lo, hi, slot, start, pos, kv_local, per_kv):
    rows, width = queries.shape
    keys = kv.shape[0]
    pairs = per_kv // 2
    block = pl.BlockSpec((TILE, per_kv * DH), lambda t, g, *_: (t, g))
    column = pl.BlockSpec((TILE, 1), lambda t, g, *_: (t, 0))
    stack = pairs * TILE
    scores_bytes = keys // TILE * stack * 2 * TILE * 4
    return pl.pallas_call(
        functools.partial(attend_kernel, pairs),
        grid_spec=pltpu.PrefetchScalarGridSpec(
            num_scalar_prefetch=3,
            grid=(rows // TILE, kv_local),
            in_specs=[block, pl.BlockSpec((keys, 2 * DH), lambda t, g, *_: (0, g)), column, column],
            out_specs=[block, block],
            scratch_shapes=[
                pltpu.VMEM((keys // TILE, stack, 2 * TILE), jnp.float32),
                pltpu.VMEM((stack, 2 * TILE), jnp.float32),
                pltpu.VMEM((stack, 2 * TILE), jnp.float32),
                pltpu.VMEM((stack, TILE), jnp.float32),
            ],
        ),
        out_shape=[
            jax.ShapeDtypeStruct((rows, width), jnp.float32),
            jax.ShapeDtypeStruct((rows, width), jnp.bfloat16),
        ],
        compiler_params=pltpu.CompilerParams(vmem_limit_bytes=scores_bytes + (16 << 20)),
        cost_estimate=pl.CostEstimate(
            flops=rows * width * keys, bytes_accessed=rows * width * 8 + keys * 512,
            transcendentals=rows * width * keys // DH // 4,
        ),
    )(lo, hi, slot, queries, kv, start, pos)


def on_device(queries, keys_values, grad_rows, doc_ids, tile_list):
    tokens_local = queries.shape[0]
    heads_local = queries.shape[1] // DH
    group = H // KVH
    kv_local = max(1, heads_local // group)
    per_kv = heads_local // kv_local
    kv_start = lax.axis_index("head") * heads_local // group
    own_kv = lax.dynamic_slice_in_dim(keys_values, kv_start * 2 * DH, kv_local * 2 * DH, 1)
    kv = lax.all_gather(own_kv, "ctx", axis=0, tiled=True)

    tile_count = tile_list.shape[0]
    tiles_local = tokens_local // TILE
    numbers = jnp.arange(tile_count, dtype=jnp.int32)
    slot = jnp.sum(jnp.where(tile_list[None, :] == numbers[:, None], numbers[None, :], 0), axis=1, dtype=jnp.int32)
    hi = lax.dynamic_slice_in_dim(tile_list, lax.axis_index("ctx") * tiles_local, tiles_local)
    docs = doc_ids.reshape(tile_count, TILE)[hi]
    start = jnp.sum(doc_ids[None, None, :] < docs[:, :, None], axis=2, dtype=jnp.int32)
    pos = hi[:, None] * TILE + jnp.arange(TILE, dtype=jnp.int32)[None, :]
    lo = start[:, 0] // TILE

    attended, low = attend(
        queries, kv, lo, hi, slot, start.reshape(-1, 1), pos.reshape(-1, 1), kv_local, per_kv
    )
    grads = lax.all_gather(grad_rows, "head", axis=1, tiled=True)
    grads = lax.all_to_all(grads, "ctx", split_axis=1, concat_axis=0, tiled=True)
    low_all = lax.all_gather(low, "ctx", axis=0, tiled=True)
    weight_grad = lax.dot_general(
        grads, low_all, (((0,), (0,)), ((), ())), preferred_element_type=jnp.float32
    )
    return (attended, weight_grad)


def solution(mesh):
    in_specs = (P("ctx", "head"), P("ctx", None), P("ctx", "head"), P(), P())
    out_specs = (P("ctx", "head"), P("ctx", "head"))
    return jax.shard_map(
        on_device, mesh=mesh, in_specs=in_specs, out_specs=out_specs, check_vma=False
    )
```

```python
import functools
import jax
import jax.numpy as jnp
from jax import lax
from jax.experimental import pallas as pl
from jax.experimental.pallas import tpu as pltpu
from jax.sharding import PartitionSpec as P

H = 64
KVH = 8
DH = 64
TILE = 128

NEG_FILL = -1e30

MESH = pl.DeviceIdType.MESH


def greet(others, head_too):
    me, n = lax.axis_index("ctx"), others
    barrier = pltpu.get_barrier_semaphore()
    for j in range(1, n):
        pl.semaphore_signal(barrier, inc=1, device_id={"ctx": lax.rem(me + j, n)}, device_id_type=MESH)
    for j in range(1, head_too):
        to = lax.rem(lax.axis_index("head") + j, head_too)
        pl.semaphore_signal(barrier, inc=1, device_id={"head": to}, device_id_type=MESH)
    pl.semaphore_wait(barrier, n - 1 + max(0, head_too - 1))


class Gather:
    def __init__(self, src, slots, send, recv, own):
        self.n = n = slots.shape[0]
        self.half = half = n // 2
        self.me = me = lax.axis_index("ctx")
        self.pair, self.side = me // 2, me % 2
        self.mate = self.pair * 2 + 1 - self.side
        self.slots, self.send, self.recv = slots, send, recv
        self.local = pltpu.make_async_copy(src, slots.at[me], own)
        self.sends = [
            self.copy(src, me, lax.rem(self.pair + j, half) * 2 + self.side, j - 1) for j in range(1, half)
        ]
        self.sends.append(self.copy(src, me, self.mate, half - 1))

    def copy(self, src, owner, to, i):
        return pltpu.make_async_remote_copy(
            src_ref=src, dst_ref=self.slots.at[owner], send_sem=self.send.at[i],
            recv_sem=self.recv.at[owner], device_id={"ctx": to}, device_id_type=MESH,
        )

    def start(self):
        for c in self.sends:
            c.start()
        self.local.start()

    def forward(self, j):
        owner = lax.rem(self.pair + self.half - j, self.half) * 2 + self.side
        c = self.copy(self.slots.at[owner], owner, self.mate, self.half - 1 + j)
        c.wait_recv()
        c.start()
        self.sends.append(c)

    def finish(self):
        self.local.wait()
        for j in range(self.half):
            owner = lax.rem(self.pair + self.half - j, self.half) * 2 + 1 - self.side
            self.copy(self.slots.at[owner], owner, self.mate, 0).wait_recv()
        for c in self.sends:
            c.wait_send()


def gather_kernel(src_ref, slots_ref, send, recv, own):
    n = slots_ref.shape[0]
    greet(n, 0)
    g = Gather(src_ref, slots_ref, send, recv, own)
    g.start()
    for j in range(1, g.half):
        g.forward(j)
    g.finish()


def gather(x, n):
    return pl.pallas_call(
        gather_kernel,
        out_shape=jax.ShapeDtypeStruct((n,) + x.shape, x.dtype),
        in_specs=[pl.BlockSpec(memory_space=pl.ANY)],
        out_specs=pl.BlockSpec(memory_space=pl.ANY),
        scratch_shapes=[
            pltpu.SemaphoreType.DMA((n - 1,)), pltpu.SemaphoreType.DMA((n,)), pltpu.SemaphoreType.DMA,
        ],
        compiler_params=pltpu.CompilerParams(collective_id=0, has_side_effects=True),
    )(x)


def grad_kernel(low_ref, g_ref, out_ref, att, spread, terms, send, recv, own,
                z_send, z_recv, z_own, a_send, a_recv, a_own):
    n, heads, halves = att.shape[0], spread.shape[0], spread.shape[1]
    me, head = lax.axis_index("ctx"), lax.axis_index("head")
    greet(n, heads)

    z_copies = [
        pltpu.make_async_remote_copy(
            src_ref=g_ref, dst_ref=spread.at[d], send_sem=z_send.at[d], recv_sem=z_recv.at[d],
            device_id={"head": lax.rem(head + d, heads)}, device_id_type=MESH,
        )
        for d in range(1, heads)
    ]
    for c in z_copies:
        c.start()
    z_local = pltpu.make_async_copy(g_ref, spread.at[0], z_own)
    z_local.start()
    g = Gather(low_ref, att, send, recv, own)
    g.start()

    def block(src, to):
        return pltpu.make_async_remote_copy(
            src_ref=src, dst_ref=terms.at[me], send_sem=a_send.at[to], recv_sem=a_recv.at[me],
            device_id={"ctx": to}, device_id_type=MESH,
        )

    def hand_out(d):
        for k in range(halves):
            to = lax.rem(head + heads - d, heads) * halves + k

            @pl.when(to != me)
            def _():
                block(spread.at[d, k], to).start()

            @pl.when(to == me)
            def _():
                pltpu.make_async_copy(spread.at[d, k], terms.at[me], a_own).start()

    z_local.wait()
    hand_out(0)
    for i in range(1, max(heads, g.half)):
        if i < g.half:
            g.forward(i)
        if i < heads:
            z_copies[i - 1].wait_recv()
            hand_out(i)
    pltpu.make_async_copy(spread.at[0, 0], terms.at[me], a_own).wait()
    for j in range(1, n):
        other = lax.rem(me + j, n)
        pltpu.make_async_remote_copy(
            src_ref=terms.at[other], dst_ref=terms.at[other], send_sem=a_send.at[other],
            recv_sem=a_recv.at[other], device_id={"ctx": other}, device_id_type=MESH,
        ).wait()
    g.finish()
    for c in z_copies:
        c.wait_send()

    count = out_ref.shape[0]
    out_ref[...] = jnp.dot(terms[0], att[0], preferred_element_type=jnp.float32)[:count]

    @pl.loop(1, n)
    def _(s):
        out_ref[...] += jnp.dot(terms[s], att[s], preferred_element_type=jnp.float32)[:count]


def grad_product(low, parts, n, heads, count):
    rows, width = low.shape
    halves, padded, _ = parts.shape
    dma = pltpu.SemaphoreType.DMA
    return pl.pallas_call(
        grad_kernel,
        out_shape=jax.ShapeDtypeStruct((count, width), jnp.float32),
        in_specs=[pl.BlockSpec(memory_space=pl.ANY)] * 2,
        out_specs=pl.BlockSpec(memory_space=pltpu.VMEM),
        scratch_shapes=[
            pltpu.VMEM((n, rows, width), low.dtype),
            pltpu.VMEM((heads, halves, padded, rows), parts.dtype),
            pltpu.VMEM((n, padded, rows), parts.dtype),
            dma((n - 1,)), dma((n,)), dma,
            dma((heads,)), dma((heads,)), dma,
            dma((n,)), dma((n,)), dma,
        ],
        compiler_params=pltpu.CompilerParams(
            collective_id=1, has_side_effects=True, vmem_limit_bytes=32 << 20,
        ),
    )(low, parts)


def attend_kernel(pairs, lo_ref, hi_ref, slot_ref, q_ref, kv_ref, start_ref, pos_ref,
                  out_ref, low_ref, s_ref, m_ref, l_ref, o_ref):
    t = pl.program_id(0)
    lo = lo_ref[t]
    hi = hi_ref[t]
    lane = lax.broadcasted_iota(jnp.int32, (TILE, TILE), 1)
    first = lane < DH
    q = jnp.concatenate(
        [q_ref[:, 2 * DH * i:2 * DH * (i + 1)] for i in range(pairs)], axis=0
    ) * jnp.bfloat16(DH ** -0.5)
    start = start_ref[...]
    pos = pos_ref[...]

    def tile_of(p):
        kv = kv_ref[pl.ds(pl.multiple_of(slot_ref[p] * TILE, TILE), TILE), :].astype(jnp.float32)
        return kv, pltpu.roll(kv, DH, 1)

    m_ref[...] = jnp.full_like(m_ref, NEG_FILL)

    @pl.loop(lo, hi + 1)
    def _(p):
        kv, swapped = tile_of(p)
        keys = jnp.concatenate(
            [jnp.where(first, kv, 0.0), jnp.where(first, 0.0, swapped)], axis=0
        ).astype(jnp.bfloat16)
        s = lax.dot_general(q, keys, (((1,), (1,)), ((), ())), preferred_element_type=jnp.float32)
        at = p * TILE + lane
        bias = jnp.where((at >= start) & (at <= pos), 0.0, NEG_FILL)
        bias = jnp.concatenate([bias, bias], axis=1)
        s = s + jnp.concatenate([bias] * pairs, axis=0)
        s_ref[p - lo] = s
        m_ref[...] = jnp.maximum(m_ref[...], s)

    m_even = jnp.max(m_ref[:, :TILE], axis=1, keepdims=True)
    m_odd = jnp.max(m_ref[:, TILE:], axis=1, keepdims=True)
    m_ref[:, :TILE] = jnp.broadcast_to(m_even, (pairs * TILE, TILE))
    m_ref[:, TILE:] = jnp.broadcast_to(m_odd, (pairs * TILE, TILE))
    l_ref[...] = jnp.zeros_like(l_ref)
    o_ref[...] = jnp.zeros_like(o_ref)

    @pl.loop(lo, hi + 1)
    def _(p):
        kv, swapped = tile_of(p)
        values = jnp.concatenate(
            [jnp.where(first, swapped, 0.0), jnp.where(first, 0.0, kv)], axis=0
        ).astype(jnp.bfloat16)
        w = jnp.exp(s_ref[p - lo] - m_ref[...])
        l_ref[...] += w
        o_ref[...] += jnp.dot(w.astype(jnp.bfloat16), values, preferred_element_type=jnp.float32)

    l_even = jnp.sum(l_ref[:, :TILE], axis=1, keepdims=True)
    l_odd = jnp.sum(l_ref[:, TILE:], axis=1, keepdims=True)
    wide = lax.broadcasted_iota(jnp.int32, (pairs * TILE, TILE), 1)
    o = o_ref[...] / jnp.where(wide < DH, l_even, l_odd)
    for i in range(pairs):
        part = o[i * TILE:(i + 1) * TILE]
        out_ref[:, 2 * DH * i:2 * DH * (i + 1)] = part
        low_ref[:, 2 * DH * i:2 * DH * (i + 1)] = part.astype(jnp.bfloat16)


def attend(queries, kv, lo, hi, slot, start, pos, kv_local, per_kv):
    rows, width = queries.shape
    keys = kv.shape[0]
    pairs = per_kv // 2
    block = pl.BlockSpec((TILE, per_kv * DH), lambda t, g, *_: (t, g))
    column = pl.BlockSpec((TILE, 1), lambda t, g, *_: (t, 0))
    stack = pairs * TILE
    scores_bytes = keys // TILE * stack * 2 * TILE * 4
    return pl.pallas_call(
        functools.partial(attend_kernel, pairs),
        grid_spec=pltpu.PrefetchScalarGridSpec(
            num_scalar_prefetch=3,
            grid=(rows // TILE, kv_local),
            in_specs=[block, pl.BlockSpec((keys, 2 * DH), lambda t, g, *_: (0, g)), column, column],
            out_specs=[block, block],
            scratch_shapes=[
                pltpu.VMEM((keys // TILE, stack, 2 * TILE), jnp.float32),
                pltpu.VMEM((stack, 2 * TILE), jnp.float32),
                pltpu.VMEM((stack, 2 * TILE), jnp.float32),
                pltpu.VMEM((stack, TILE), jnp.float32),
            ],
        ),
        out_shape=[
            jax.ShapeDtypeStruct((rows, width), jnp.float32),
            jax.ShapeDtypeStruct((rows, width), jnp.bfloat16),
        ],
        compiler_params=pltpu.CompilerParams(vmem_limit_bytes=scores_bytes + (16 << 20)),
        cost_estimate=pl.CostEstimate(
            flops=rows * width * keys, bytes_accessed=rows * width * 8 + keys * 512,
            transcendentals=rows * width * keys // DH // 4,
        ),
    )(lo, hi, slot, queries, kv, start, pos)


def on_device(queries, keys_values, grad_rows, doc_ids, tile_list):
    tokens_local = queries.shape[0]
    heads_local = queries.shape[1] // DH
    group = H // KVH
    kv_local = max(1, heads_local // group)
    per_kv = heads_local // kv_local
    kv_start = lax.axis_index("head") * heads_local // group
    own_kv = lax.dynamic_slice_in_dim(keys_values, kv_start * 2 * DH, kv_local * 2 * DH, 1)
    n, heads = lax.axis_size("ctx"), lax.axis_size("head")
    kv = gather(own_kv, n).reshape(n * tokens_local, -1)

    tile_count = tile_list.shape[0]
    tiles_local = tokens_local // TILE
    numbers = jnp.arange(tile_count, dtype=jnp.int32)
    slot = jnp.sum(jnp.where(tile_list[None, :] == numbers[:, None], numbers[None, :], 0), axis=1, dtype=jnp.int32)
    hi = lax.dynamic_slice_in_dim(tile_list, lax.axis_index("ctx") * tiles_local, tiles_local)
    docs = doc_ids.reshape(tile_count, TILE)[hi]
    start = jnp.sum(doc_ids[None, None, :] < docs[:, :, None], axis=2, dtype=jnp.int32)
    pos = hi[:, None] * TILE + jnp.arange(TILE, dtype=jnp.int32)[None, :]
    lo = start[:, 0] // TILE

    attended, low = attend(
        queries, kv, lo, hi, slot, start.reshape(-1, 1), pos.reshape(-1, 1), kv_local, per_kv
    )
    count = grad_rows.shape[1] * heads // n
    parts = grad_rows.T.reshape(n // heads, count, tokens_local)
    parts = jnp.pad(parts, ((0, 0), (0, -count % 16), (0, 0)))
    weight_grad = grad_product(low, parts, n, heads, count)
    return (attended, weight_grad)


def solution(mesh):
    in_specs = (P("ctx", "head"), P("ctx", None), P("ctx", "head"), P(), P())
    out_specs = (P("ctx", "head"), P("ctx", "head"))
    return jax.shard_map(
        on_device, mesh=mesh, in_specs=in_specs, out_specs=out_specs, check_vma=False
    )
```

```python
import functools
import jax
import jax.numpy as jnp
from jax import lax
from jax.experimental import pallas as pl
from jax.experimental.pallas import tpu as pltpu
from jax.sharding import PartitionSpec as P

H = 64
KVH = 8
DH = 64
TILE = 128

NEG_FILL = -1e30

MESH = pl.DeviceIdType.MESH


def greet(others, head_too):
    me, n = lax.axis_index("ctx"), others
    barrier = pltpu.get_barrier_semaphore()
    for j in range(1, n):
        pl.semaphore_signal(barrier, inc=1, device_id={"ctx": lax.rem(me + j, n)}, device_id_type=MESH)
    for j in range(1, head_too):
        to = lax.rem(lax.axis_index("head") + j, head_too)
        pl.semaphore_signal(barrier, inc=1, device_id={"head": to}, device_id_type=MESH)
    pl.semaphore_wait(barrier, n - 1 + max(0, head_too - 1))


class Gather:
    def __init__(self, src, slots, send, recv, own):
        self.n = n = slots.shape[0]
        self.half = half = n // 2
        self.me = me = lax.axis_index("ctx")
        self.pair, self.side = me // 2, me % 2
        self.mate = self.pair * 2 + 1 - self.side
        self.slots, self.send, self.recv = slots, send, recv
        self.local = pltpu.make_async_copy(src, slots.at[me], own)
        self.sends = [
            self.copy(src, me, lax.rem(self.pair + j, half) * 2 + self.side, j - 1) for j in range(1, half)
        ]
        self.sends.append(self.copy(src, me, self.mate, half - 1))

    def copy(self, src, owner, to, i):
        return pltpu.make_async_remote_copy(
            src_ref=src, dst_ref=self.slots.at[owner], send_sem=self.send.at[i],
            recv_sem=self.recv.at[owner], device_id={"ctx": to}, device_id_type=MESH,
        )

    def start(self):
        for c in self.sends:
            c.start()
        self.local.start()

    def forward(self, j):
        owner = lax.rem(self.pair + self.half - j, self.half) * 2 + self.side
        c = self.copy(self.slots.at[owner], owner, self.mate, self.half - 1 + j)
        c.wait_recv()
        c.start()
        self.sends.append(c)

    def finish(self):
        self.local.wait()
        for j in range(self.half):
            owner = lax.rem(self.pair + self.half - j, self.half) * 2 + 1 - self.side
            self.copy(self.slots.at[owner], owner, self.mate, 0).wait_recv()
        for c in self.sends:
            c.wait_send()


class Spread:
    def __init__(self, parts_of, slots, terms, right, left, recv, a_send, a_recv, a_own):
        self.heads, self.halves, self.n = slots.shape[0], slots.shape[1], terms.shape[0]
        self.parts_of, self.slots, self.terms = parts_of, slots, terms
        self.right, self.left, self.recv = right, left, recv
        self.a_send, self.a_recv, self.a_own = a_send, a_recv, a_own
        self.me, self.head = lax.axis_index("ctx"), lax.axis_index("head")

    def hop_copy(self, i, owner, to, send):
        return pltpu.make_async_remote_copy(
            src_ref=self.parts_of(i - 1, owner), dst_ref=self.slots.at[owner], send_sem=send.at[i],
            recv_sem=self.recv.at[owner], device_id={"head": to}, device_id_type=MESH,
        )

    def each_sent(self, i, act):
        head, heads = self.head, self.heads
        to_right, to_left = head - (i - 1), head + (i - 1)

        @pl.when((to_right >= 0) & (head + 1 < heads))
        def _():
            act(self.hop_copy(i, to_right, head + 1, self.right))

        @pl.when((to_left < heads) & (head >= 1))
        def _():
            act(self.hop_copy(i, to_left, head - 1, self.left))

    def start_hop(self, i):
        self.each_sent(i, lambda c: c.start())

    def end_hop(self, i):
        self.each_sent(i, lambda c: c.wait_send())

    def each_owner(self, i, act):
        if i == 0:
            act(self.head)
            return

        @pl.when(self.head >= i)
        def _():
            act(self.head - i)

        @pl.when(self.head + i < self.heads)
        def _():
            act(self.head + i)

    def arrive(self, i):
        def wait(owner):
            pltpu.make_async_remote_copy(
                src_ref=self.slots.at[owner], dst_ref=self.slots.at[owner], send_sem=self.right.at[i],
                recv_sem=self.recv.at[owner], device_id={"head": owner}, device_id_type=MESH,
            ).wait_recv()

        self.each_owner(i, wait)

    def each_block(self, i, remote, local):
        def blocks(owner):
            for k in range(self.halves):
                to = owner * self.halves + k
                src = self.parts_of(i, owner).at[k]

                @pl.when(to != self.me)
                def _():
                    remote(pltpu.make_async_remote_copy(
                        src_ref=src, dst_ref=self.terms.at[self.me], send_sem=self.a_send.at[to],
                        recv_sem=self.a_recv.at[self.me], device_id={"ctx": to}, device_id_type=MESH,
                    ))

                @pl.when(to == self.me)
                def _():
                    local(pltpu.make_async_copy(src, self.terms.at[self.me], self.a_own))

        self.each_owner(i, blocks)

    def hand_out(self, i):
        self.each_block(i, lambda c: c.start(), lambda c: c.start())

    def end_hand_out(self, i):
        self.each_block(i, lambda c: c.wait_send(), lambda c: c.wait())

    def wait_terms(self):
        for j in range(1, self.n):
            other = lax.rem(self.me + j, self.n)
            pltpu.make_async_remote_copy(
                src_ref=self.terms.at[other], dst_ref=self.terms.at[other], send_sem=self.a_send.at[other],
                recv_sem=self.a_recv.at[other], device_id={"ctx": other}, device_id_type=MESH,
            ).wait_recv()


def is_near(halves):
    gap = lax.axis_index("head") - lax.axis_index("ctx") // halves
    return (gap <= 1) & (gap >= -1)


def first_kernel(kv_ref, g_ref, all_ref, slots_ref, terms_ref, send, recv, own,
                 right, left, z_recv, a_send, a_recv, a_own):
    n, heads, halves = all_ref.shape[0], slots_ref.shape[0], slots_ref.shape[1]
    greet(n, heads)
    sp = Spread(
        lambda i, owner: g_ref if i == 0 else slots_ref.at[owner],
        slots_ref, terms_ref, right, left, z_recv, a_send, a_recv, a_own,
    )
    g = Gather(kv_ref, all_ref, send, recv, own)
    hops = min(2, heads - 1)
    g.start()
    sp.start_hop(1)
    sp.hand_out(0)
    for j in range(1, g.half):
        g.forward(j)
    for i in range(1, hops + 1):
        sp.arrive(i)
        if i < hops:
            sp.start_hop(i + 1)
        if i == 1:
            sp.hand_out(1)

    @pl.when(is_near(halves))
    def _():
        sp.wait_terms()

    for i in (0, 1):
        sp.end_hand_out(i)
    for i in range(1, hops + 1):
        sp.end_hop(i)
    g.finish()


def spread_sems(n, heads):
    dma = pltpu.SemaphoreType.DMA
    return [
        dma((n - 1,)), dma((n,)), dma,
        dma((heads,)), dma((heads,)), dma((heads,)),
        dma((n,)), dma((n,)), dma,
    ]


def first_moves(kv, parts, n, heads):
    whole = pl.BlockSpec(memory_space=pl.ANY)
    halves, padded, rows = parts.shape
    return pl.pallas_call(
        first_kernel,
        out_shape=[
            jax.ShapeDtypeStruct((n,) + kv.shape, kv.dtype),
            jax.ShapeDtypeStruct((heads,) + parts.shape, parts.dtype),
            jax.ShapeDtypeStruct((n, padded, rows), parts.dtype),
        ],
        in_specs=[whole] * 2,
        out_specs=[whole] * 3,
        scratch_shapes=spread_sems(n, heads),
        compiler_params=pltpu.CompilerParams(collective_id=0, has_side_effects=True),
    )(kv, parts)


def grad_kernel(low_ref, early_ref, near_ref, out_ref, att, slots, terms, copied, send, recv, own,
                right, left, z_recv, a_send, a_recv, a_own):
    n, heads, halves = att.shape[0], slots.shape[0], slots.shape[1]
    greet(n, heads)
    sp = Spread(
        lambda i, owner: (early_ref if i <= 2 else slots).at[owner],
        slots, terms, right, left, z_recv, a_send, a_recv, a_own,
    )
    g = Gather(low_ref, att, send, recv, own)
    near = is_near(halves)
    if heads > 3:
        sp.start_hop(3)
    if heads > 2:
        sp.hand_out(2)
    g.start()

    @pl.when(near)
    def _():
        pltpu.make_async_copy(near_ref, terms, copied).start()

    for i in range(1, max(heads - 2, g.half)):
        if i < g.half:
            g.forward(i)
        if i + 2 < heads:
            sp.arrive(i + 2)
            if i + 3 < heads:
                sp.start_hop(i + 3)
            sp.hand_out(i + 2)

    @pl.when(near)
    def _():
        pltpu.make_async_copy(near_ref, terms, copied).wait()

    for i in range(2, heads):
        sp.end_hand_out(i)

    @pl.when(jnp.logical_not(near))
    def _():
        sp.wait_terms()

    for i in range(3, heads):
        sp.end_hop(i)
    g.finish()

    count = out_ref.shape[0]
    out_ref[...] = jnp.dot(terms[0], att[0], preferred_element_type=jnp.float32)[:count]

    @pl.loop(1, n)
    def _(s):
        out_ref[...] += jnp.dot(terms[s], att[s], preferred_element_type=jnp.float32)[:count]


def grad_product(low, early, near, count):
    rows, width = low.shape
    heads, n = early.shape[0], near.shape[0]
    whole = pl.BlockSpec(memory_space=pl.ANY)
    return pl.pallas_call(
        grad_kernel,
        out_shape=jax.ShapeDtypeStruct((count, width), jnp.float32),
        in_specs=[whole] * 3,
        out_specs=pl.BlockSpec(memory_space=pltpu.VMEM),
        scratch_shapes=[
            pltpu.VMEM((n, rows, width), low.dtype),
            pltpu.VMEM(early.shape, early.dtype),
            pltpu.VMEM(near.shape, near.dtype),
            pltpu.SemaphoreType.DMA,
        ] + spread_sems(n, heads),
        compiler_params=pltpu.CompilerParams(
            collective_id=1, has_side_effects=True, vmem_limit_bytes=32 << 20,
        ),
    )(low, early, near)


def attend_kernel(pairs, lo_ref, hi_ref, slot_ref, q_ref, kv_ref, start_ref, pos_ref,
                  out_ref, low_ref, s_ref, m_ref, l_ref, o_ref):
    t = pl.program_id(0)
    lo = lo_ref[t]
    hi = hi_ref[t]
    lane = lax.broadcasted_iota(jnp.int32, (TILE, TILE), 1)
    first = lane < DH
    q = jnp.concatenate(
        [q_ref[:, 2 * DH * i:2 * DH * (i + 1)] for i in range(pairs)], axis=0
    ) * jnp.bfloat16(DH ** -0.5)
    start = start_ref[...]
    pos = pos_ref[...]

    def tile_of(p):
        kv = kv_ref[pl.ds(pl.multiple_of(slot_ref[p] * TILE, TILE), TILE), :].astype(jnp.float32)
        return kv, pltpu.roll(kv, DH, 1)

    m_ref[...] = jnp.full_like(m_ref, NEG_FILL)

    @pl.loop(lo, hi + 1)
    def _(p):
        kv, swapped = tile_of(p)
        keys = jnp.concatenate(
            [jnp.where(first, kv, 0.0), jnp.where(first, 0.0, swapped)], axis=0
        ).astype(jnp.bfloat16)
        s = lax.dot_general(q, keys, (((1,), (1,)), ((), ())), preferred_element_type=jnp.float32)
        at = p * TILE + lane
        bias = jnp.where((at >= start) & (at <= pos), 0.0, NEG_FILL)
        bias = jnp.concatenate([bias, bias], axis=1)
        s = s + jnp.concatenate([bias] * pairs, axis=0)
        s_ref[p - lo] = s
        m_ref[...] = jnp.maximum(m_ref[...], s)

    m_even = jnp.max(m_ref[:, :TILE], axis=1, keepdims=True)
    m_odd = jnp.max(m_ref[:, TILE:], axis=1, keepdims=True)
    m_ref[:, :TILE] = jnp.broadcast_to(m_even, (pairs * TILE, TILE))
    m_ref[:, TILE:] = jnp.broadcast_to(m_odd, (pairs * TILE, TILE))
    l_ref[...] = jnp.zeros_like(l_ref)
    o_ref[...] = jnp.zeros_like(o_ref)

    @pl.loop(lo, hi + 1)
    def _(p):
        kv, swapped = tile_of(p)
        values = jnp.concatenate(
            [jnp.where(first, swapped, 0.0), jnp.where(first, 0.0, kv)], axis=0
        ).astype(jnp.bfloat16)
        w = jnp.exp(s_ref[p - lo] - m_ref[...])
        l_ref[...] += w
        o_ref[...] += jnp.dot(w.astype(jnp.bfloat16), values, preferred_element_type=jnp.float32)

    l_even = jnp.sum(l_ref[:, :TILE], axis=1, keepdims=True)
    l_odd = jnp.sum(l_ref[:, TILE:], axis=1, keepdims=True)
    wide = lax.broadcasted_iota(jnp.int32, (pairs * TILE, TILE), 1)
    o = o_ref[...] / jnp.where(wide < DH, l_even, l_odd)
    for i in range(pairs):
        part = o[i * TILE:(i + 1) * TILE]
        out_ref[:, 2 * DH * i:2 * DH * (i + 1)] = part
        low_ref[:, 2 * DH * i:2 * DH * (i + 1)] = part.astype(jnp.bfloat16)


def attend(queries, kv, lo, hi, slot, start, pos, kv_local, per_kv):
    rows, width = queries.shape
    keys = kv.shape[0]
    pairs = per_kv // 2
    block = pl.BlockSpec((TILE, per_kv * DH), lambda t, g, *_: (t, g))
    column = pl.BlockSpec((TILE, 1), lambda t, g, *_: (t, 0))
    stack = pairs * TILE
    scores_bytes = keys // TILE * stack * 2 * TILE * 4
    return pl.pallas_call(
        functools.partial(attend_kernel, pairs),
        grid_spec=pltpu.PrefetchScalarGridSpec(
            num_scalar_prefetch=3,
            grid=(rows // TILE, kv_local),
            in_specs=[block, pl.BlockSpec((keys, 2 * DH), lambda t, g, *_: (0, g)), column, column],
            out_specs=[block, block],
            scratch_shapes=[
                pltpu.VMEM((keys // TILE, stack, 2 * TILE), jnp.float32),
                pltpu.VMEM((stack, 2 * TILE), jnp.float32),
                pltpu.VMEM((stack, 2 * TILE), jnp.float32),
                pltpu.VMEM((stack, TILE), jnp.float32),
            ],
        ),
        out_shape=[
            jax.ShapeDtypeStruct((rows, width), jnp.float32),
            jax.ShapeDtypeStruct((rows, width), jnp.bfloat16),
        ],
        compiler_params=pltpu.CompilerParams(vmem_limit_bytes=scores_bytes + (16 << 20)),
        cost_estimate=pl.CostEstimate(
            flops=rows * width * keys, bytes_accessed=rows * width * 8 + keys * 512,
            transcendentals=rows * width * keys // DH // 4,
        ),
    )(lo, hi, slot, queries, kv, start, pos)


def on_device(queries, keys_values, grad_rows, doc_ids, tile_list):
    tokens_local = queries.shape[0]
    heads_local = queries.shape[1] // DH
    group = H // KVH
    kv_local = max(1, heads_local // group)
    per_kv = heads_local // kv_local
    kv_start = lax.axis_index("head") * heads_local // group
    own_kv = lax.dynamic_slice_in_dim(keys_values, kv_start * 2 * DH, kv_local * 2 * DH, 1)
    n, heads = lax.axis_size("ctx"), lax.axis_size("head")
    count = grad_rows.shape[1] * heads // n
    parts = grad_rows.T.reshape(n // heads, count, tokens_local)
    parts = jnp.pad(parts, ((0, 0), (0, -count % 16), (0, 0)))
    kv, early, near = first_moves(own_kv, parts, n, heads)
    kv = kv.reshape(n * tokens_local, -1)

    tile_count = tile_list.shape[0]
    tiles_local = tokens_local // TILE
    numbers = jnp.arange(tile_count, dtype=jnp.int32)
    slot = jnp.sum(jnp.where(tile_list[None, :] == numbers[:, None], numbers[None, :], 0), axis=1, dtype=jnp.int32)
    hi = lax.dynamic_slice_in_dim(tile_list, lax.axis_index("ctx") * tiles_local, tiles_local)
    docs = doc_ids.reshape(tile_count, TILE)[hi]
    start = jnp.sum(doc_ids[None, None, :] < docs[:, :, None], axis=2, dtype=jnp.int32)
    pos = hi[:, None] * TILE + jnp.arange(TILE, dtype=jnp.int32)[None, :]
    lo = start[:, 0] // TILE

    attended, low = attend(
        queries, kv, lo, hi, slot, start.reshape(-1, 1), pos.reshape(-1, 1), kv_local, per_kv
    )
    weight_grad = grad_product(low, early, near, count)
    return (attended, weight_grad)


def solution(mesh):
    in_specs = (P("ctx", "head"), P("ctx", None), P("ctx", "head"), P(), P())
    out_specs = (P("ctx", "head"), P("ctx", "head"))
    return jax.shard_map(
        on_device, mesh=mesh, in_specs=in_specs, out_specs=out_specs, check_vma=False
    )
```

```python
import functools
import jax
import jax.numpy as jnp
from jax import lax
from jax.experimental import pallas as pl
from jax.experimental.pallas import tpu as pltpu
from jax.sharding import PartitionSpec as P

H = 64
KVH = 8
DH = 64
TILE = 128

NEG_FILL = -1e30

MESH = pl.DeviceIdType.MESH


def greet(others, head_too):
    me, n = lax.axis_index("ctx"), others
    barrier = pltpu.get_barrier_semaphore()
    for j in range(1, n):
        pl.semaphore_signal(barrier, inc=1, device_id={"ctx": lax.rem(me + j, n)}, device_id_type=MESH)
    for j in range(1, head_too):
        to = lax.rem(lax.axis_index("head") + j, head_too)
        pl.semaphore_signal(barrier, inc=1, device_id={"head": to}, device_id_type=MESH)
    pl.semaphore_wait(barrier, n - 1 + max(0, head_too - 1))


class Gather:
    def __init__(self, src, slots, send, recv, own):
        self.n = n = slots.shape[0]
        self.half = half = n // 2
        self.me = me = lax.axis_index("ctx")
        self.pair, self.side = me // 2, me % 2
        self.mate = self.pair * 2 + 1 - self.side
        self.slots, self.send, self.recv = slots, send, recv
        self.local = pltpu.make_async_copy(src, slots.at[me], own)
        if half == 4:
            pair = self.pair
            self.near = (pair + 1 - 2 * (pair % 2)) * 2 + self.side
            self.next = lax.rem(pair + 2, 4) * 2 + self.side
            self.far = (3 - pair) * 2 + self.side
            targets = [self.near, self.next]
        else:
            targets = [lax.rem(self.pair + j, half) * 2 + self.side for j in range(1, half)]
        self.sends = [self.copy(src, me, to, i) for i, to in enumerate(targets)]
        self.sends.append(self.copy(src, me, self.mate, half - 1))

    def copy(self, src, owner, to, i):
        return pltpu.make_async_remote_copy(
            src_ref=src, dst_ref=self.slots.at[owner], send_sem=self.send.at[i],
            recv_sem=self.recv.at[owner], device_id={"ctx": to}, device_id_type=MESH,
        )

    def part(self, owner, which, to, i):
        rows = self.slots.shape[1] // 2
        ref = self.slots.at[owner, pl.ds(which * rows, rows)]
        return pltpu.make_async_remote_copy(
            src_ref=ref, dst_ref=ref, send_sem=self.send.at[i],
            recv_sem=self.recv.at[owner + which * self.n], device_id={"ctx": to}, device_id_type=MESH,
        )

    def start(self):
        for c in self.sends:
            c.start()
        self.local.start()

    def square(self, j):
        if j < 3:
            owner, to = (self.near, self.next) if j == 1 else (self.next, self.near)
            c = self.copy(self.slots.at[owner], owner, self.mate, 3 + j)
            c.wait_recv()
            half = self.part(owner, j - 1, to, 6 + j)
            half.start()
            self.sends.append(half)
        else:
            owner = self.far
            for which in range(2):
                self.part(owner, which, self.mate, 0).wait_recv()
            c = self.copy(self.slots.at[owner], owner, self.mate, 3 + j)
        c.start()
        self.sends.append(c)

    def forward(self, j):
        if self.half == 4:
            self.square(j)
            return
        owner = lax.rem(self.pair + self.half - j, self.half) * 2 + self.side
        c = self.copy(self.slots.at[owner], owner, self.mate, self.half - 1 + j)
        c.wait_recv()
        c.start()
        self.sends.append(c)

    def finish(self):
        self.local.wait()
        for j in range(self.half):
            owner = lax.rem(self.pair + self.half - j, self.half) * 2 + 1 - self.side
            self.copy(self.slots.at[owner], owner, self.mate, 0).wait_recv()
        for c in self.sends:
            c.wait_send()


class Spread:
    def __init__(self, parts_of, slots, terms, right, left, recv, a_send, a_recv, a_own):
        self.heads, self.halves, self.n = slots.shape[0], slots.shape[1], terms.shape[0]
        self.parts_of, self.slots, self.terms = parts_of, slots, terms
        self.right, self.left, self.recv = right, left, recv
        self.a_send, self.a_recv, self.a_own = a_send, a_recv, a_own
        self.me, self.head = lax.axis_index("ctx"), lax.axis_index("head")

    def hop_copy(self, i, owner, to, send):
        return pltpu.make_async_remote_copy(
            src_ref=self.parts_of(i - 1, owner), dst_ref=self.slots.at[owner], send_sem=send.at[i],
            recv_sem=self.recv.at[owner], device_id={"head": to}, device_id_type=MESH,
        )

    def each_sent(self, i, act):
        head, heads = self.head, self.heads
        to_right, to_left = head - (i - 1), head + (i - 1)

        @pl.when((to_right >= 0) & (head + 1 < heads))
        def _():
            act(self.hop_copy(i, to_right, head + 1, self.right))

        @pl.when((to_left < heads) & (head >= 1))
        def _():
            act(self.hop_copy(i, to_left, head - 1, self.left))

    def start_hop(self, i):
        self.each_sent(i, lambda c: c.start())

    def end_hop(self, i):
        self.each_sent(i, lambda c: c.wait_send())

    def each_owner(self, i, act):
        if i == 0:
            act(self.head)
            return

        @pl.when(self.head >= i)
        def _():
            act(self.head - i)

        @pl.when(self.head + i < self.heads)
        def _():
            act(self.head + i)

    def arrive(self, i):
        def wait(owner):
            pltpu.make_async_remote_copy(
                src_ref=self.slots.at[owner], dst_ref=self.slots.at[owner], send_sem=self.right.at[i],
                recv_sem=self.recv.at[owner], device_id={"head": owner}, device_id_type=MESH,
            ).wait_recv()

        self.each_owner(i, wait)

    def each_block(self, i, remote, local):
        def blocks(owner):
            for k in range(self.halves):
                to = owner * self.halves + k
                src = self.parts_of(i, owner).at[k]

                @pl.when(to != self.me)
                def _():
                    remote(pltpu.make_async_remote_copy(
                        src_ref=src, dst_ref=self.terms.at[self.me], send_sem=self.a_send.at[to],
                        recv_sem=self.a_recv.at[self.me], device_id={"ctx": to}, device_id_type=MESH,
                    ))

                @pl.when(to == self.me)
                def _():
                    local(pltpu.make_async_copy(src, self.terms.at[self.me], self.a_own))

        self.each_owner(i, blocks)

    def hand_out(self, i):
        self.each_block(i, lambda c: c.start(), lambda c: c.start())

    def end_hand_out(self, i):
        self.each_block(i, lambda c: c.wait_send(), lambda c: c.wait())

    def wait_terms(self):
        for j in range(1, self.n):
            other = lax.rem(self.me + j, self.n)
            pltpu.make_async_remote_copy(
                src_ref=self.terms.at[other], dst_ref=self.terms.at[other], send_sem=self.a_send.at[other],
                recv_sem=self.a_recv.at[other], device_id={"ctx": other}, device_id_type=MESH,
            ).wait_recv()


def is_near(halves):
    gap = lax.axis_index("head") - lax.axis_index("ctx") // halves
    return gap == 0


def first_kernel(kv_ref, g_ref, all_ref, slots_ref, terms_ref, send, recv, own,
                 right, left, z_recv, a_send, a_recv, a_own):
    n, heads, halves = all_ref.shape[0], slots_ref.shape[0], slots_ref.shape[1]
    greet(n, heads)
    sp = Spread(
        lambda i, owner: g_ref if i == 0 else slots_ref.at[owner],
        slots_ref, terms_ref, right, left, z_recv, a_send, a_recv, a_own,
    )
    g = Gather(kv_ref, all_ref, send, recv, own)
    g.start()
    sp.start_hop(1)
    sp.hand_out(0)
    for j in range(1, g.half):
        g.forward(j)
    sp.arrive(1)

    @pl.when(is_near(halves))
    def _():
        sp.wait_terms()

    sp.end_hand_out(0)
    sp.end_hop(1)
    g.finish()


def spread_sems(n, heads):
    dma = pltpu.SemaphoreType.DMA
    return [
        dma((2 * n,)), dma((2 * n,)), dma,
        dma((heads,)), dma((heads,)), dma((heads,)),
        dma((n,)), dma((n,)), dma,
    ]


def first_moves(kv, parts, n, heads):
    whole = pl.BlockSpec(memory_space=pl.ANY)
    halves, padded, rows = parts.shape
    return pl.pallas_call(
        first_kernel,
        out_shape=[
            jax.ShapeDtypeStruct((n,) + kv.shape, kv.dtype),
            jax.ShapeDtypeStruct((heads,) + parts.shape, parts.dtype),
            jax.ShapeDtypeStruct((n, padded, rows), parts.dtype),
        ],
        in_specs=[whole] * 2,
        out_specs=[whole] * 3,
        scratch_shapes=spread_sems(n, heads),
        compiler_params=pltpu.CompilerParams(collective_id=0, has_side_effects=True),
    )(kv, parts)


def grad_kernel(low_ref, early_ref, near_ref, out_ref, att, slots, terms, copied, send, recv, own,
                right, left, z_recv, a_send, a_recv, a_own):
    n, heads, halves = att.shape[0], slots.shape[0], slots.shape[1]
    greet(n, heads)
    sp = Spread(
        lambda i, owner: (early_ref if i <= 1 else slots).at[owner],
        slots, terms, right, left, z_recv, a_send, a_recv, a_own,
    )
    g = Gather(low_ref, att, send, recv, own)
    near = is_near(halves)
    g.start()
    sp.start_hop(2)
    sp.hand_out(1)

    @pl.when(near)
    def _():
        pltpu.make_async_copy(near_ref, terms, copied).start()

    for i in range(1, max(heads - 1, g.half)):
        if i + 1 < heads:
            sp.arrive(i + 1)
            if i + 2 < heads:
                sp.start_hop(i + 2)
            sp.hand_out(i + 1)
        if i < g.half:
            g.forward(i)

    @pl.when(near)
    def _():
        pltpu.make_async_copy(near_ref, terms, copied).wait()

    for i in range(1, heads):
        sp.end_hand_out(i)

    @pl.when(jnp.logical_not(near))
    def _():
        sp.wait_terms()

    for i in range(2, heads):
        sp.end_hop(i)
    g.finish()

    count = out_ref.shape[0]
    out_ref[...] = jnp.dot(terms[0], att[0], preferred_element_type=jnp.float32)[:count]

    @pl.loop(1, n)
    def _(s):
        out_ref[...] += jnp.dot(terms[s], att[s], preferred_element_type=jnp.float32)[:count]


def grad_product(low, early, near, count):
    rows, width = low.shape
    heads, n = early.shape[0], near.shape[0]
    whole = pl.BlockSpec(memory_space=pl.ANY)
    return pl.pallas_call(
        grad_kernel,
        out_shape=jax.ShapeDtypeStruct((count, width), jnp.float32),
        in_specs=[whole] * 3,
        out_specs=pl.BlockSpec(memory_space=pltpu.VMEM),
        scratch_shapes=[
            pltpu.VMEM((n, rows, width), low.dtype),
            pltpu.VMEM(early.shape, early.dtype),
            pltpu.VMEM(near.shape, near.dtype),
            pltpu.SemaphoreType.DMA,
        ] + spread_sems(n, heads),
        compiler_params=pltpu.CompilerParams(
            collective_id=1, has_side_effects=True, vmem_limit_bytes=32 << 20,
        ),
    )(low, early, near)


def attend_kernel(pairs, lo_ref, hi_ref, slot_ref, q_ref, kv_ref, start_ref, pos_ref,
                  out_ref, low_ref, s_ref, m_ref, l_ref, o_ref):
    t = pl.program_id(0)
    lo = lo_ref[t]
    hi = hi_ref[t]
    lane = lax.broadcasted_iota(jnp.int32, (TILE, TILE), 1)
    first = lane < DH
    q = jnp.concatenate(
        [q_ref[:, 2 * DH * i:2 * DH * (i + 1)] for i in range(pairs)], axis=0
    ) * jnp.bfloat16(DH ** -0.5)
    start = start_ref[...]
    pos = pos_ref[...]

    def tile_of(p):
        kv = kv_ref[pl.ds(pl.multiple_of(slot_ref[p] * TILE, TILE), TILE), :].astype(jnp.float32)
        return kv, pltpu.roll(kv, DH, 1)

    m_ref[...] = jnp.full_like(m_ref, NEG_FILL)

    @pl.loop(lo, hi + 1)
    def _(p):
        kv, swapped = tile_of(p)
        keys = jnp.concatenate(
            [jnp.where(first, kv, 0.0), jnp.where(first, 0.0, swapped)], axis=0
        ).astype(jnp.bfloat16)
        s = lax.dot_general(q, keys, (((1,), (1,)), ((), ())), preferred_element_type=jnp.float32)
        at = p * TILE + lane
        bias = jnp.where((at >= start) & (at <= pos), 0.0, NEG_FILL)
        bias = jnp.concatenate([bias, bias], axis=1)
        s = s + jnp.concatenate([bias] * pairs, axis=0)
        s_ref[p - lo] = s
        m_ref[...] = jnp.maximum(m_ref[...], s)

    m_even = jnp.max(m_ref[:, :TILE], axis=1, keepdims=True)
    m_odd = jnp.max(m_ref[:, TILE:], axis=1, keepdims=True)
    m_ref[:, :TILE] = jnp.broadcast_to(m_even, (pairs * TILE, TILE))
    m_ref[:, TILE:] = jnp.broadcast_to(m_odd, (pairs * TILE, TILE))
    l_ref[...] = jnp.zeros_like(l_ref)
    o_ref[...] = jnp.zeros_like(o_ref)

    @pl.loop(lo, hi + 1)
    def _(p):
        kv, swapped = tile_of(p)
        values = jnp.concatenate(
            [jnp.where(first, swapped, 0.0), jnp.where(first, 0.0, kv)], axis=0
        ).astype(jnp.bfloat16)
        w = jnp.exp(s_ref[p - lo] - m_ref[...])
        l_ref[...] += w
        o_ref[...] += jnp.dot(w.astype(jnp.bfloat16), values, preferred_element_type=jnp.float32)

    l_even = jnp.sum(l_ref[:, :TILE], axis=1, keepdims=True)
    l_odd = jnp.sum(l_ref[:, TILE:], axis=1, keepdims=True)
    wide = lax.broadcasted_iota(jnp.int32, (pairs * TILE, TILE), 1)
    o = o_ref[...] / jnp.where(wide < DH, l_even, l_odd)
    for i in range(pairs):
        part = o[i * TILE:(i + 1) * TILE]
        out_ref[:, 2 * DH * i:2 * DH * (i + 1)] = part
        low_ref[:, 2 * DH * i:2 * DH * (i + 1)] = part.astype(jnp.bfloat16)


def attend(queries, kv, lo, hi, slot, start, pos, kv_local, per_kv):
    rows, width = queries.shape
    keys = kv.shape[0]
    pairs = per_kv // 2
    block = pl.BlockSpec((TILE, per_kv * DH), lambda t, g, *_: (t, g))
    column = pl.BlockSpec((TILE, 1), lambda t, g, *_: (t, 0))
    stack = pairs * TILE
    scores_bytes = keys // TILE * stack * 2 * TILE * 4
    return pl.pallas_call(
        functools.partial(attend_kernel, pairs),
        grid_spec=pltpu.PrefetchScalarGridSpec(
            num_scalar_prefetch=3,
            grid=(rows // TILE, kv_local),
            in_specs=[block, pl.BlockSpec((keys, 2 * DH), lambda t, g, *_: (0, g)), column, column],
            out_specs=[block, block],
            scratch_shapes=[
                pltpu.VMEM((keys // TILE, stack, 2 * TILE), jnp.float32),
                pltpu.VMEM((stack, 2 * TILE), jnp.float32),
                pltpu.VMEM((stack, 2 * TILE), jnp.float32),
                pltpu.VMEM((stack, TILE), jnp.float32),
            ],
        ),
        out_shape=[
            jax.ShapeDtypeStruct((rows, width), jnp.float32),
            jax.ShapeDtypeStruct((rows, width), jnp.bfloat16),
        ],
        compiler_params=pltpu.CompilerParams(vmem_limit_bytes=scores_bytes + (16 << 20)),
        cost_estimate=pl.CostEstimate(
            flops=rows * width * keys, bytes_accessed=rows * width * 8 + keys * 512,
            transcendentals=rows * width * keys // DH // 4,
        ),
    )(lo, hi, slot, queries, kv, start, pos)


def on_device(queries, keys_values, grad_rows, doc_ids, tile_list):
    tokens_local = queries.shape[0]
    heads_local = queries.shape[1] // DH
    group = H // KVH
    kv_local = max(1, heads_local // group)
    per_kv = heads_local // kv_local
    kv_start = lax.axis_index("head") * heads_local // group
    own_kv = lax.dynamic_slice_in_dim(keys_values, kv_start * 2 * DH, kv_local * 2 * DH, 1)
    n, heads = lax.axis_size("ctx"), lax.axis_size("head")
    count = grad_rows.shape[1] * heads // n
    parts = grad_rows.T.reshape(n // heads, count, tokens_local)
    parts = jnp.pad(parts, ((0, 0), (0, -count % 16), (0, 0)))
    kv, early, near = first_moves(own_kv, parts, n, heads)
    kv = kv.reshape(n * tokens_local, -1)

    tile_count = tile_list.shape[0]
    tiles_local = tokens_local // TILE
    numbers = jnp.arange(tile_count, dtype=jnp.int32)
    slot = jnp.sum(jnp.where(tile_list[None, :] == numbers[:, None], numbers[None, :], 0), axis=1, dtype=jnp.int32)
    hi = lax.dynamic_slice_in_dim(tile_list, lax.axis_index("ctx") * tiles_local, tiles_local)
    docs = doc_ids.reshape(tile_count, TILE)[hi]
    start = jnp.sum(doc_ids[None, None, :] < docs[:, :, None], axis=2, dtype=jnp.int32)
    pos = hi[:, None] * TILE + jnp.arange(TILE, dtype=jnp.int32)[None, :]
    lo = start[:, 0] // TILE

    attended, low = attend(
        queries, kv, lo, hi, slot, start.reshape(-1, 1), pos.reshape(-1, 1), kv_local, per_kv
    )
    weight_grad = grad_product(low, early, near, count)
    return (attended, weight_grad)


def solution(mesh):
    in_specs = (P("ctx", "head"), P("ctx", None), P("ctx", "head"), P(), P())
    out_specs = (P("ctx", "head"), P("ctx", "head"))
    return jax.shard_map(
        on_device, mesh=mesh, in_specs=in_specs, out_specs=out_specs, check_vma=False
    )
```

```python
import functools
import jax
import jax.numpy as jnp
from jax import lax
from jax.experimental import pallas as pl
from jax.experimental.pallas import tpu as pltpu
from jax.sharding import PartitionSpec as P

H = 64
KVH = 8
DH = 64
TILE = 128

NEG_FILL = -1e30

MESH = pl.DeviceIdType.MESH


def greet(others, head_too):
    me, n = lax.axis_index("ctx"), others
    barrier = pltpu.get_barrier_semaphore()
    for j in range(1, n):
        pl.semaphore_signal(barrier, inc=1, device_id={"ctx": lax.rem(me + j, n)}, device_id_type=MESH)
    for j in range(1, head_too):
        to = lax.rem(lax.axis_index("head") + j, head_too)
        pl.semaphore_signal(barrier, inc=1, device_id={"head": to}, device_id_type=MESH)
    pl.semaphore_wait(barrier, n - 1 + max(0, head_too - 1))


class Gather:
    def __init__(self, src, slots, send, recv, own):
        self.n = n = slots.shape[0]
        self.half = half = n // 2
        self.me = me = lax.axis_index("ctx")
        self.pair, self.side = me // 2, me % 2
        self.mate = self.pair * 2 + 1 - self.side
        self.slots, self.send, self.recv = slots, send, recv
        self.local = pltpu.make_async_copy(src, slots.at[me], own)
        if half == 4:
            pair = self.pair
            self.near = (pair + 1 - 2 * (pair % 2)) * 2 + self.side
            self.next = lax.rem(pair + 2, 4) * 2 + self.side
            self.far = (3 - pair) * 2 + self.side
            targets = [self.near, self.next]
        else:
            targets = [lax.rem(self.pair + j, half) * 2 + self.side for j in range(1, half)]
        self.sends = [self.copy(src, me, to, i) for i, to in enumerate(targets)]
        self.sends.append(self.copy(src, me, self.mate, half - 1))

    def copy(self, src, owner, to, i):
        return pltpu.make_async_remote_copy(
            src_ref=src, dst_ref=self.slots.at[owner], send_sem=self.send.at[i],
            recv_sem=self.recv.at[owner], device_id={"ctx": to}, device_id_type=MESH,
        )

    def part(self, owner, which, to, i):
        rows = self.slots.shape[1] // 2
        ref = self.slots.at[owner, pl.ds(which * rows, rows)]
        return pltpu.make_async_remote_copy(
            src_ref=ref, dst_ref=ref, send_sem=self.send.at[i],
            recv_sem=self.recv.at[owner + which * self.n], device_id={"ctx": to}, device_id_type=MESH,
        )

    def start(self):
        for c in self.sends:
            c.start()
        self.local.start()

    def square(self, j):
        if j < 3:
            owner, to = (self.near, self.next) if j == 1 else (self.next, self.near)
            c = self.copy(self.slots.at[owner], owner, self.mate, 3 + j)
            c.wait_recv()
            half = self.part(owner, j - 1, to, 6 + j)
            half.start()
            self.sends.append(half)
        else:
            owner = self.far
            for which in range(2):
                self.part(owner, which, self.mate, 0).wait_recv()
            c = self.copy(self.slots.at[owner], owner, self.mate, 3 + j)
        c.start()
        self.sends.append(c)

    def forward(self, j):
        if self.half == 4:
            self.square(j)
            return
        owner = lax.rem(self.pair + self.half - j, self.half) * 2 + self.side
        c = self.copy(self.slots.at[owner], owner, self.mate, self.half - 1 + j)
        c.wait_recv()
        c.start()
        self.sends.append(c)

    def finish(self):
        self.local.wait()
        for j in range(self.half):
            owner = lax.rem(self.pair + self.half - j, self.half) * 2 + 1 - self.side
            self.copy(self.slots.at[owner], owner, self.mate, 0).wait_recv()
        for c in self.sends:
            c.wait_send()


class Spread:
    def __init__(self, parts_of, slots, terms, right, left, recv, a_send, a_recv, a_own):
        self.heads, self.halves, self.n = slots.shape[0], slots.shape[1], lax.axis_size("ctx")
        self.parts_of, self.slots, self.terms = parts_of, slots, terms
        self.right, self.left, self.recv = right, left, recv
        self.a_send, self.a_recv, self.a_own = a_send, a_recv, a_own
        self.me, self.head = lax.axis_index("ctx"), lax.axis_index("head")

    def hop_copy(self, i, owner, to, send):
        return pltpu.make_async_remote_copy(
            src_ref=self.parts_of(i - 1, owner), dst_ref=self.slots.at[owner], send_sem=send.at[i],
            recv_sem=self.recv.at[owner], device_id={"head": to}, device_id_type=MESH,
        )

    def each_sent(self, i, act):
        head, heads = self.head, self.heads
        to_right, to_left = head - (i - 1), head + (i - 1)

        @pl.when((to_right >= 0) & (head + 1 < heads))
        def _():
            act(self.hop_copy(i, to_right, head + 1, self.right))

        @pl.when((to_left < heads) & (head >= 1))
        def _():
            act(self.hop_copy(i, to_left, head - 1, self.left))

    def start_hop(self, i):
        self.each_sent(i, lambda c: c.start())

    def end_hop(self, i):
        self.each_sent(i, lambda c: c.wait_send())

    def each_owner(self, i, act):
        if i == 0:
            act(self.head)
            return

        @pl.when(self.head >= i)
        def _():
            act(self.head - i)

        @pl.when(self.head + i < self.heads)
        def _():
            act(self.head + i)

    def arrive(self, i):
        def wait(owner):
            pltpu.make_async_remote_copy(
                src_ref=self.slots.at[owner], dst_ref=self.slots.at[owner], send_sem=self.right.at[i],
                recv_sem=self.recv.at[owner], device_id={"head": owner}, device_id_type=MESH,
            ).wait_recv()

        self.each_owner(i, wait)

    def each_block(self, i, remote, local):
        def blocks(owner):
            for k in range(self.halves):
                to = owner * self.halves + k
                src = self.parts_of(i, owner).at[k]

                @pl.when(to != self.me)
                def _():
                    remote(pltpu.make_async_remote_copy(
                        src_ref=src, dst_ref=self.terms.at[self.me], send_sem=self.a_send.at[to],
                        recv_sem=self.a_recv.at[self.me], device_id={"ctx": to}, device_id_type=MESH,
                    ))

                @pl.when(to == self.me)
                def _():
                    local(pltpu.make_async_copy(src, self.terms.at[self.me], self.a_own))

        self.each_owner(i, blocks)

    def hand_out(self, i):
        self.each_block(i, lambda c: c.start(), lambda c: c.start())

    def end_hand_out(self, i):
        self.each_block(i, lambda c: c.wait_send(), lambda c: c.wait())

    def wait_terms(self):
        for j in range(1, self.n):
            other = lax.rem(self.me + j, self.n)
            pltpu.make_async_remote_copy(
                src_ref=self.terms.at[other], dst_ref=self.terms.at[other], send_sem=self.a_send.at[other],
                recv_sem=self.a_recv.at[other], device_id={"ctx": other}, device_id_type=MESH,
            ).wait_recv()


def first_kernel(kv_ref, g_ref, all_ref, slots_ref, send, recv, own, right, left, z_recv):
    n, heads = all_ref.shape[0], slots_ref.shape[0]
    greet(n, heads)
    sp = Spread(
        lambda i, owner: g_ref if i == 0 else slots_ref.at[owner],
        slots_ref, None, right, left, z_recv, None, None, None,
    )
    g = Gather(kv_ref, all_ref, send, recv, own)
    g.start()
    sp.start_hop(1)
    for j in range(1, g.half):
        g.forward(j)
    sp.arrive(1)
    sp.end_hop(1)
    g.finish()


def spread_sems(n, heads):
    dma = pltpu.SemaphoreType.DMA
    return [
        dma((2 * n,)), dma((2 * n,)), dma,
        dma((heads,)), dma((heads,)), dma((heads,)),
        dma((n,)), dma((n,)), dma,
    ]


def first_moves(kv, parts, n, heads):
    whole = pl.BlockSpec(memory_space=pl.ANY)
    return pl.pallas_call(
        first_kernel,
        out_shape=[
            jax.ShapeDtypeStruct((n,) + kv.shape, kv.dtype),
            jax.ShapeDtypeStruct((heads,) + parts.shape, parts.dtype),
        ],
        in_specs=[whole] * 2,
        out_specs=[whole] * 2,
        scratch_shapes=spread_sems(n, heads)[:6],
        compiler_params=pltpu.CompilerParams(collective_id=0, has_side_effects=True),
    )(kv, parts)


def grad_kernel(low_ref, g_ref, early_ref, out_ref, att, slots, terms, send, recv, own,
                right, left, z_recv, a_send, a_recv, a_own):
    n, heads = att.shape[0], slots.shape[0]
    greet(n, heads)
    sp = Spread(
        lambda i, owner: g_ref if i == 0 else (early_ref if i == 1 else slots).at[owner],
        slots, terms, right, left, z_recv, a_send, a_recv, a_own,
    )
    g = Gather(low_ref, att, send, recv, own)
    g.start()
    sp.start_hop(2)
    sp.hand_out(0)
    sp.hand_out(1)

    for i in range(1, max(heads - 1, g.half)):
        if i + 1 < heads:
            sp.arrive(i + 1)
            if i + 2 < heads:
                sp.start_hop(i + 2)
            sp.hand_out(i + 1)
        if i < g.half:
            g.forward(i)

    for i in range(heads):
        sp.end_hand_out(i)
    sp.wait_terms()

    for i in range(2, heads):
        sp.end_hop(i)
    g.finish()

    count = out_ref.shape[0]
    out_ref[...] = jnp.dot(terms[0], att[0], preferred_element_type=jnp.float32)[:count]

    @pl.loop(1, n)
    def _(s):
        out_ref[...] += jnp.dot(terms[s], att[s], preferred_element_type=jnp.float32)[:count]


def grad_product(low, parts, early, n, count):
    rows, width = low.shape
    heads, _, padded, _ = early.shape
    whole = pl.BlockSpec(memory_space=pl.ANY)
    return pl.pallas_call(
        grad_kernel,
        out_shape=jax.ShapeDtypeStruct((count, width), jnp.float32),
        in_specs=[whole] * 3,
        out_specs=pl.BlockSpec(memory_space=pltpu.VMEM),
        scratch_shapes=[
            pltpu.VMEM((n, rows, width), low.dtype),
            pltpu.VMEM(early.shape, early.dtype),
            pltpu.VMEM((n, padded, rows), early.dtype),
        ] + spread_sems(n, heads),
        compiler_params=pltpu.CompilerParams(
            collective_id=1, has_side_effects=True, vmem_limit_bytes=32 << 20,
        ),
    )(low, parts, early)


def attend_kernel(pairs, lo_ref, hi_ref, slot_ref, q_ref, kv_ref, start_ref, pos_ref,
                  out_ref, low_ref, s_ref, m_ref, l_ref, o_ref):
    t = pl.program_id(0)
    lo = lo_ref[t]
    hi = hi_ref[t]
    lane = lax.broadcasted_iota(jnp.int32, (TILE, TILE), 1)
    first = lane < DH
    q = jnp.concatenate(
        [q_ref[:, 2 * DH * i:2 * DH * (i + 1)] for i in range(pairs)], axis=0
    ) * jnp.bfloat16(DH ** -0.5)
    start = start_ref[...]
    pos = pos_ref[...]

    def tile_of(p):
        kv = kv_ref[pl.ds(pl.multiple_of(slot_ref[p] * TILE, TILE), TILE), :].astype(jnp.float32)
        return kv, pltpu.roll(kv, DH, 1)

    m_ref[...] = jnp.full_like(m_ref, NEG_FILL)

    @pl.loop(lo, hi + 1)
    def _(p):
        kv, swapped = tile_of(p)
        keys = jnp.concatenate(
            [jnp.where(first, kv, 0.0), jnp.where(first, 0.0, swapped)], axis=0
        ).astype(jnp.bfloat16)
        s = lax.dot_general(q, keys, (((1,), (1,)), ((), ())), preferred_element_type=jnp.float32)
        at = p * TILE + lane
        bias = jnp.where((at >= start) & (at <= pos), 0.0, NEG_FILL)
        bias = jnp.concatenate([bias, bias], axis=1)
        s = s + jnp.concatenate([bias] * pairs, axis=0)
        s_ref[p - lo] = s
        m_ref[...] = jnp.maximum(m_ref[...], s)

    m_even = jnp.max(m_ref[:, :TILE], axis=1, keepdims=True)
    m_odd = jnp.max(m_ref[:, TILE:], axis=1, keepdims=True)
    m_ref[:, :TILE] = jnp.broadcast_to(m_even, (pairs * TILE, TILE))
    m_ref[:, TILE:] = jnp.broadcast_to(m_odd, (pairs * TILE, TILE))
    l_ref[...] = jnp.zeros_like(l_ref)
    o_ref[...] = jnp.zeros_like(o_ref)

    @pl.loop(lo, hi + 1)
    def _(p):
        kv, swapped = tile_of(p)
        values = jnp.concatenate(
            [jnp.where(first, swapped, 0.0), jnp.where(first, 0.0, kv)], axis=0
        ).astype(jnp.bfloat16)
        w = jnp.exp(s_ref[p - lo] - m_ref[...])
        l_ref[...] += w
        o_ref[...] += jnp.dot(w.astype(jnp.bfloat16), values, preferred_element_type=jnp.float32)

    l_even = jnp.sum(l_ref[:, :TILE], axis=1, keepdims=True)
    l_odd = jnp.sum(l_ref[:, TILE:], axis=1, keepdims=True)
    wide = lax.broadcasted_iota(jnp.int32, (pairs * TILE, TILE), 1)
    o = o_ref[...] / jnp.where(wide < DH, l_even, l_odd)
    for i in range(pairs):
        part = o[i * TILE:(i + 1) * TILE]
        out_ref[:, 2 * DH * i:2 * DH * (i + 1)] = part
        low_ref[:, 2 * DH * i:2 * DH * (i + 1)] = part.astype(jnp.bfloat16)


def attend(queries, kv, lo, hi, slot, start, pos, kv_local, per_kv):
    rows, width = queries.shape
    keys = kv.shape[0]
    pairs = per_kv // 2
    block = pl.BlockSpec((TILE, per_kv * DH), lambda t, g, *_: (t, g))
    column = pl.BlockSpec((TILE, 1), lambda t, g, *_: (t, 0))
    stack = pairs * TILE
    scores_bytes = keys // TILE * stack * 2 * TILE * 4
    return pl.pallas_call(
        functools.partial(attend_kernel, pairs),
        grid_spec=pltpu.PrefetchScalarGridSpec(
            num_scalar_prefetch=3,
            grid=(rows // TILE, kv_local),
            in_specs=[block, pl.BlockSpec((keys, 2 * DH), lambda t, g, *_: (0, g)), column, column],
            out_specs=[block, block],
            scratch_shapes=[
                pltpu.VMEM((keys // TILE, stack, 2 * TILE), jnp.float32),
                pltpu.VMEM((stack, 2 * TILE), jnp.float32),
                pltpu.VMEM((stack, 2 * TILE), jnp.float32),
                pltpu.VMEM((stack, TILE), jnp.float32),
            ],
        ),
        out_shape=[
            jax.ShapeDtypeStruct((rows, width), jnp.float32),
            jax.ShapeDtypeStruct((rows, width), jnp.bfloat16),
        ],
        compiler_params=pltpu.CompilerParams(vmem_limit_bytes=scores_bytes + (16 << 20)),
        cost_estimate=pl.CostEstimate(
            flops=rows * width * keys, bytes_accessed=rows * width * 8 + keys * 512,
            transcendentals=rows * width * keys // DH // 4,
        ),
    )(lo, hi, slot, queries, kv, start, pos)


def on_device(queries, keys_values, grad_rows, doc_ids, tile_list):
    tokens_local = queries.shape[0]
    heads_local = queries.shape[1] // DH
    group = H // KVH
    kv_local = max(1, heads_local // group)
    per_kv = heads_local // kv_local
    kv_start = lax.axis_index("head") * heads_local // group
    own_kv = lax.dynamic_slice_in_dim(keys_values, kv_start * 2 * DH, kv_local * 2 * DH, 1)
    n, heads = lax.axis_size("ctx"), lax.axis_size("head")
    count = grad_rows.shape[1] * heads // n
    parts = grad_rows.T.reshape(n // heads, count, tokens_local)
    parts = jnp.pad(parts, ((0, 0), (0, -count % 16), (0, 0)))
    kv, early = first_moves(own_kv, parts, n, heads)
    kv = kv.reshape(n * tokens_local, -1)

    tile_count = tile_list.shape[0]
    tiles_local = tokens_local // TILE
    numbers = jnp.arange(tile_count, dtype=jnp.int32)
    slot = jnp.sum(jnp.where(tile_list[None, :] == numbers[:, None], numbers[None, :], 0), axis=1, dtype=jnp.int32)
    hi = lax.dynamic_slice_in_dim(tile_list, lax.axis_index("ctx") * tiles_local, tiles_local)
    docs = doc_ids.reshape(tile_count, TILE)[hi]
    start = jnp.sum(doc_ids[None, None, :] < docs[:, :, None], axis=2, dtype=jnp.int32)
    pos = hi[:, None] * TILE + jnp.arange(TILE, dtype=jnp.int32)[None, :]
    lo = start[:, 0] // TILE

    attended, low = attend(
        queries, kv, lo, hi, slot, start.reshape(-1, 1), pos.reshape(-1, 1), kv_local, per_kv
    )
    weight_grad = grad_product(low, parts, early, n, count)
    return (attended, weight_grad)


def solution(mesh):
    in_specs = (P("ctx", "head"), P("ctx", None), P("ctx", "head"), P(), P())
    out_specs = (P("ctx", "head"), P("ctx", "head"))
    return jax.shard_map(
        on_device, mesh=mesh, in_specs=in_specs, out_specs=out_specs, check_vma=False
    )
```

```python
import functools
import jax
import jax.numpy as jnp
from jax import lax
from jax.experimental import pallas as pl
from jax.experimental.pallas import tpu as pltpu
from jax.sharding import PartitionSpec as P

H = 64
KVH = 8
DH = 64
TILE = 128

NEG_FILL = -1e30

MESH = pl.DeviceIdType.MESH


def greet(others, head_too):
    me, n = lax.axis_index("ctx"), others
    barrier = pltpu.get_barrier_semaphore()
    for j in range(1, n):
        pl.semaphore_signal(barrier, inc=1, device_id={"ctx": lax.rem(me + j, n)}, device_id_type=MESH)
    for j in range(1, head_too):
        to = lax.rem(lax.axis_index("head") + j, head_too)
        pl.semaphore_signal(barrier, inc=1, device_id={"head": to}, device_id_type=MESH)
    pl.semaphore_wait(barrier, n - 1 + max(0, head_too - 1))


class Gather:
    def __init__(self, src, slots, send, recv, own):
        self.n = n = slots.shape[0]
        self.half = half = n // 2
        self.me = me = lax.axis_index("ctx")
        self.pair, self.side = me // 2, me % 2
        self.mate = self.pair * 2 + 1 - self.side
        self.slots, self.send, self.recv = slots, send, recv
        self.local = pltpu.make_async_copy(src, slots.at[me], own)
        if half == 4:
            pair = self.pair
            self.near = (pair + 1 - 2 * (pair % 2)) * 2 + self.side
            self.next = lax.rem(pair + 2, 4) * 2 + self.side
            self.far = (3 - pair) * 2 + self.side
            targets = [self.near, self.next]
        else:
            targets = [lax.rem(self.pair + j, half) * 2 + self.side for j in range(1, half)]
        self.sends = [self.copy(src, me, to, i) for i, to in enumerate(targets)]
        self.sends.append(self.copy(src, me, self.mate, half - 1))

    def copy(self, src, owner, to, i):
        return pltpu.make_async_remote_copy(
            src_ref=src, dst_ref=self.slots.at[owner], send_sem=self.send.at[i],
            recv_sem=self.recv.at[owner], device_id={"ctx": to}, device_id_type=MESH,
        )

    def part(self, owner, which, to, i):
        rows = self.slots.shape[1] // 2
        ref = self.slots.at[owner, pl.ds(which * rows, rows)]
        return pltpu.make_async_remote_copy(
            src_ref=ref, dst_ref=ref, send_sem=self.send.at[i],
            recv_sem=self.recv.at[owner + which * self.n], device_id={"ctx": to}, device_id_type=MESH,
        )

    def start(self):
        for c in self.sends:
            c.start()
        self.local.start()

    def square(self, j):
        if j < 3:
            owner, to = (self.near, self.next) if j == 1 else (self.next, self.near)
            c = self.copy(self.slots.at[owner], owner, self.mate, 3 + j)
            c.wait_recv()
            half = self.part(owner, j - 1, to, 6 + j)
            half.start()
            self.sends.append(half)
        else:
            owner = self.far
            for which in range(2):
                self.part(owner, which, self.mate, 0).wait_recv()
            c = self.copy(self.slots.at[owner], owner, self.mate, 3 + j)
        c.start()
        self.sends.append(c)

    def forward(self, j):
        if self.half == 4:
            self.square(j)
            return
        owner = lax.rem(self.pair + self.half - j, self.half) * 2 + self.side
        c = self.copy(self.slots.at[owner], owner, self.mate, self.half - 1 + j)
        c.wait_recv()
        c.start()
        self.sends.append(c)

    def finish(self):
        self.local.wait()
        for j in range(self.half):
            owner = lax.rem(self.pair + self.half - j, self.half) * 2 + 1 - self.side
            self.copy(self.slots.at[owner], owner, self.mate, 0).wait_recv()
        for c in self.sends:
            c.wait_send()


class Spread:
    def __init__(self, parts_of, slots, terms, right, left, recv, a_send, a_recv, a_own):
        self.heads, self.halves, self.n = slots.shape[0], slots.shape[1], lax.axis_size("ctx")
        self.parts_of, self.slots, self.terms = parts_of, slots, terms
        self.right, self.left, self.recv = right, left, recv
        self.a_send, self.a_recv, self.a_own = a_send, a_recv, a_own
        self.me, self.head = lax.axis_index("ctx"), lax.axis_index("head")

    def hop_copy(self, i, owner, to, send):
        return pltpu.make_async_remote_copy(
            src_ref=self.parts_of(i - 1, owner), dst_ref=self.slots.at[owner], send_sem=send.at[i],
            recv_sem=self.recv.at[owner], device_id={"head": to}, device_id_type=MESH,
        )

    def each_sent(self, i, act):
        head, heads = self.head, self.heads
        to_right, to_left = head - (i - 1), head + (i - 1)

        @pl.when((to_right >= 0) & (head + 1 < heads))
        def _():
            act(self.hop_copy(i, to_right, head + 1, self.right))

        @pl.when((to_left < heads) & (head >= 1))
        def _():
            act(self.hop_copy(i, to_left, head - 1, self.left))

    def start_hop(self, i):
        self.each_sent(i, lambda c: c.start())

    def end_hop(self, i):
        self.each_sent(i, lambda c: c.wait_send())

    def each_owner(self, i, act):
        if i == 0:
            act(self.head)
            return

        @pl.when(self.head >= i)
        def _():
            act(self.head - i)

        @pl.when(self.head + i < self.heads)
        def _():
            act(self.head + i)

    def arrive(self, i):
        def wait(owner):
            pltpu.make_async_remote_copy(
                src_ref=self.slots.at[owner], dst_ref=self.slots.at[owner], send_sem=self.right.at[i],
                recv_sem=self.recv.at[owner], device_id={"head": owner}, device_id_type=MESH,
            ).wait_recv()

        self.each_owner(i, wait)

    def each_block(self, i, remote, local):
        def blocks(owner):
            for k in range(self.halves):
                to = owner * self.halves + k
                src = self.parts_of(i, owner).at[k]

                @pl.when(to != self.me)
                def _():
                    remote(pltpu.make_async_remote_copy(
                        src_ref=src, dst_ref=self.terms.at[self.me], send_sem=self.a_send.at[to],
                        recv_sem=self.a_recv.at[self.me], device_id={"ctx": to}, device_id_type=MESH,
                    ))

                @pl.when(to == self.me)
                def _():
                    local(pltpu.make_async_copy(src, self.terms.at[self.me], self.a_own))

        self.each_owner(i, blocks)

    def hand_out(self, i):
        self.each_block(i, lambda c: c.start(), lambda c: c.start())

    def end_hand_out(self, i):
        self.each_block(i, lambda c: c.wait_send(), lambda c: c.wait())

    def wait_terms(self):
        for j in range(1, self.n):
            other = lax.rem(self.me + j, self.n)
            pltpu.make_async_remote_copy(
                src_ref=self.terms.at[other], dst_ref=self.terms.at[other], send_sem=self.a_send.at[other],
                recv_sem=self.a_recv.at[other], device_id={"ctx": other}, device_id_type=MESH,
            ).wait_recv()


def first_kernel(kv_ref, g_ref, all_ref, slots_ref, send, recv, own, right, left, z_recv):
    n, heads = all_ref.shape[0], slots_ref.shape[0]
    greet(n, heads)
    sp = Spread(
        lambda i, owner: g_ref if i == 0 else slots_ref.at[owner],
        slots_ref, None, right, left, z_recv, None, None, None,
    )
    g = Gather(kv_ref, all_ref, send, recv, own)
    g.start()
    sp.start_hop(1)
    for j in range(1, g.half):
        g.forward(j)
    sp.arrive(1)
    sp.end_hop(1)
    g.finish()


def spread_sems(n, heads):
    dma = pltpu.SemaphoreType.DMA
    return [
        dma((2 * n,)), dma((2 * n,)), dma,
        dma((heads,)), dma((heads,)), dma((heads,)),
        dma((n,)), dma((n,)), dma,
    ]


def first_moves(kv, parts, n, heads):
    whole = pl.BlockSpec(memory_space=pl.ANY)
    return pl.pallas_call(
        first_kernel,
        out_shape=[
            jax.ShapeDtypeStruct((n,) + kv.shape, kv.dtype),
            jax.ShapeDtypeStruct((heads,) + parts.shape, parts.dtype),
        ],
        in_specs=[whole] * 2,
        out_specs=[whole] * 2,
        scratch_shapes=spread_sems(n, heads)[:6],
        compiler_params=pltpu.CompilerParams(collective_id=0, has_side_effects=True),
    )(kv, parts)


def grad_kernel(low_ref, g_ref, early_ref, out_ref, att, slots, terms, send, recv, own,
                right, left, z_recv, a_send, a_recv, a_own):
    n, heads = att.shape[0], slots.shape[0]
    greet(n, heads)
    sp = Spread(
        lambda i, owner: g_ref if i == 0 else (early_ref if i == 1 else slots).at[owner],
        slots, terms, right, left, z_recv, a_send, a_recv, a_own,
    )
    g = Gather(low_ref, att, send, recv, own)
    g.start()
    sp.start_hop(2)
    sp.hand_out(0)
    sp.hand_out(1)

    for i in range(1, max(heads - 1, g.half)):
        if 1 < i < g.half:
            g.forward(i)
        if i + 1 < heads:
            sp.arrive(i + 1)
            if i + 2 < heads:
                sp.start_hop(i + 2)
            sp.hand_out(i + 1)
        if i == 1 and i < g.half:
            g.forward(i)

    for i in range(heads):
        sp.end_hand_out(i)
    sp.wait_terms()

    for i in range(2, heads):
        sp.end_hop(i)
    g.finish()

    count = out_ref.shape[0]
    out_ref[...] = jnp.dot(terms[0], att[0], preferred_element_type=jnp.float32)[:count]

    @pl.loop(1, n)
    def _(s):
        out_ref[...] += jnp.dot(terms[s], att[s], preferred_element_type=jnp.float32)[:count]


def grad_product(low, parts, early, n, count):
    rows, width = low.shape
    heads, _, padded, _ = early.shape
    whole = pl.BlockSpec(memory_space=pl.ANY)
    return pl.pallas_call(
        grad_kernel,
        out_shape=jax.ShapeDtypeStruct((count, width), jnp.float32),
        in_specs=[whole] * 3,
        out_specs=pl.BlockSpec(memory_space=pltpu.VMEM),
        scratch_shapes=[
            pltpu.VMEM((n, rows, width), low.dtype),
            pltpu.VMEM(early.shape, early.dtype),
            pltpu.VMEM((n, padded, rows), early.dtype),
        ] + spread_sems(n, heads),
        compiler_params=pltpu.CompilerParams(
            collective_id=1, has_side_effects=True, vmem_limit_bytes=32 << 20,
        ),
    )(low, parts, early)


def attend_kernel(pairs, lo_ref, hi_ref, slot_ref, q_ref, kv_ref, start_ref, pos_ref,
                  out_ref, low_ref, s_ref, m_ref, l_ref, o_ref):
    t = pl.program_id(0)
    lo = lo_ref[t]
    hi = hi_ref[t]
    lane = lax.broadcasted_iota(jnp.int32, (TILE, TILE), 1)
    first = lane < DH
    q = jnp.concatenate(
        [q_ref[:, 2 * DH * i:2 * DH * (i + 1)] for i in range(pairs)], axis=0
    ) * jnp.bfloat16(DH ** -0.5)
    start = start_ref[...]
    pos = pos_ref[...]

    def tile_of(p):
        kv = kv_ref[pl.ds(pl.multiple_of(slot_ref[p] * TILE, TILE), TILE), :].astype(jnp.float32)
        return kv, pltpu.roll(kv, DH, 1)

    m_ref[...] = jnp.full_like(m_ref, NEG_FILL)

    @pl.loop(lo, hi + 1)
    def _(p):
        kv, swapped = tile_of(p)
        keys = jnp.concatenate(
            [jnp.where(first, kv, 0.0), jnp.where(first, 0.0, swapped)], axis=0
        ).astype(jnp.bfloat16)
        s = lax.dot_general(q, keys, (((1,), (1,)), ((), ())), preferred_element_type=jnp.float32)
        at = p * TILE + lane
        bias = jnp.where((at >= start) & (at <= pos), 0.0, NEG_FILL)
        bias = jnp.concatenate([bias, bias], axis=1)
        s = s + jnp.concatenate([bias] * pairs, axis=0)
        s_ref[p - lo] = s
        m_ref[...] = jnp.maximum(m_ref[...], s)

    m_even = jnp.max(m_ref[:, :TILE], axis=1, keepdims=True)
    m_odd = jnp.max(m_ref[:, TILE:], axis=1, keepdims=True)
    m_ref[:, :TILE] = jnp.broadcast_to(m_even, (pairs * TILE, TILE))
    m_ref[:, TILE:] = jnp.broadcast_to(m_odd, (pairs * TILE, TILE))
    l_ref[...] = jnp.zeros_like(l_ref)
    o_ref[...] = jnp.zeros_like(o_ref)

    @pl.loop(lo, hi + 1)
    def _(p):
        kv, swapped = tile_of(p)
        values = jnp.concatenate(
            [jnp.where(first, swapped, 0.0), jnp.where(first, 0.0, kv)], axis=0
        ).astype(jnp.bfloat16)
        w = jnp.exp(s_ref[p - lo] - m_ref[...])
        l_ref[...] += w
        o_ref[...] += jnp.dot(w.astype(jnp.bfloat16), values, preferred_element_type=jnp.float32)

    l_even = jnp.sum(l_ref[:, :TILE], axis=1, keepdims=True)
    l_odd = jnp.sum(l_ref[:, TILE:], axis=1, keepdims=True)
    wide = lax.broadcasted_iota(jnp.int32, (pairs * TILE, TILE), 1)
    o = o_ref[...] / jnp.where(wide < DH, l_even, l_odd)
    for i in range(pairs):
        part = o[i * TILE:(i + 1) * TILE]
        out_ref[:, 2 * DH * i:2 * DH * (i + 1)] = part
        low_ref[:, 2 * DH * i:2 * DH * (i + 1)] = part.astype(jnp.bfloat16)


def attend(queries, kv, lo, hi, slot, start, pos, kv_local, per_kv):
    rows, width = queries.shape
    keys = kv.shape[0]
    pairs = per_kv // 2
    block = pl.BlockSpec((TILE, per_kv * DH), lambda t, g, *_: (t, g))
    column = pl.BlockSpec((TILE, 1), lambda t, g, *_: (t, 0))
    stack = pairs * TILE
    scores_bytes = keys // TILE * stack * 2 * TILE * 4
    return pl.pallas_call(
        functools.partial(attend_kernel, pairs),
        grid_spec=pltpu.PrefetchScalarGridSpec(
            num_scalar_prefetch=3,
            grid=(rows // TILE, kv_local),
            in_specs=[block, pl.BlockSpec((keys, 2 * DH), lambda t, g, *_: (0, g)), column, column],
            out_specs=[block, block],
            scratch_shapes=[
                pltpu.VMEM((keys // TILE, stack, 2 * TILE), jnp.float32),
                pltpu.VMEM((stack, 2 * TILE), jnp.float32),
                pltpu.VMEM((stack, 2 * TILE), jnp.float32),
                pltpu.VMEM((stack, TILE), jnp.float32),
            ],
        ),
        out_shape=[
            jax.ShapeDtypeStruct((rows, width), jnp.float32),
            jax.ShapeDtypeStruct((rows, width), jnp.bfloat16),
        ],
        compiler_params=pltpu.CompilerParams(vmem_limit_bytes=scores_bytes + (16 << 20)),
        cost_estimate=pl.CostEstimate(
            flops=rows * width * keys, bytes_accessed=rows * width * 8 + keys * 512,
            transcendentals=rows * width * keys // DH // 4,
        ),
    )(lo, hi, slot, queries, kv, start, pos)


def on_device(queries, keys_values, grad_rows, doc_ids, tile_list):
    tokens_local = queries.shape[0]
    heads_local = queries.shape[1] // DH
    group = H // KVH
    kv_local = max(1, heads_local // group)
    per_kv = heads_local // kv_local
    kv_start = lax.axis_index("head") * heads_local // group
    own_kv = lax.dynamic_slice_in_dim(keys_values, kv_start * 2 * DH, kv_local * 2 * DH, 1)
    n, heads = lax.axis_size("ctx"), lax.axis_size("head")
    count = grad_rows.shape[1] * heads // n
    parts = grad_rows.T.reshape(n // heads, count, tokens_local)
    parts = jnp.pad(parts, ((0, 0), (0, -count % 16), (0, 0)))
    kv, early = first_moves(own_kv, parts, n, heads)
    kv = kv.reshape(n * tokens_local, -1)

    tile_count = tile_list.shape[0]
    tiles_local = tokens_local // TILE
    numbers = jnp.arange(tile_count, dtype=jnp.int32)
    slot = jnp.sum(jnp.where(tile_list[None, :] == numbers[:, None], numbers[None, :], 0), axis=1, dtype=jnp.int32)
    hi = lax.dynamic_slice_in_dim(tile_list, lax.axis_index("ctx") * tiles_local, tiles_local)
    docs = doc_ids.reshape(tile_count, TILE)[hi]
    start = jnp.sum(doc_ids[None, None, :] < docs[:, :, None], axis=2, dtype=jnp.int32)
    pos = hi[:, None] * TILE + jnp.arange(TILE, dtype=jnp.int32)[None, :]
    lo = start[:, 0] // TILE

    attended, low = attend(
        queries, kv, lo, hi, slot, start.reshape(-1, 1), pos.reshape(-1, 1), kv_local, per_kv
    )
    weight_grad = grad_product(low, parts, early, n, count)
    return (attended, weight_grad)


def solution(mesh):
    in_specs = (P("ctx", "head"), P("ctx", None), P("ctx", "head"), P(), P())
    out_specs = (P("ctx", "head"), P("ctx", "head"))
    return jax.shard_map(
        on_device, mesh=mesh, in_specs=in_specs, out_specs=out_specs, check_vma=False
    )
```
